512 devices in a mesh: pair: 2 (over core), tensor: 16 (over z), vocab: 16 (over x, y).
Axes of the slice: x: 4, y: 4, z: 16, core: 2. Of those that a mesh axis runs over, the one named last changes fastest.
Arguments:
- context: bfloat16 [2, 512, 8192], P('pair', 'vocab', 'tensor'), may hold values from -6 to 6
- residual: bfloat16 [2, 512, 8192], P('pair', 'tensor', 'vocab')
- out_weight: bfloat16 [8192, 8192], P('tensor', 'vocab'), may hold values from -0.0625 to 0.0625
- norm_gain: float32 [8192], P('vocab'), may hold values from 0.1 to 1.9
- head_weight: bfloat16 [8192, 65536], P(None, ('tensor', 'vocab'))
- partner: int32 [512], replicated, may hold values from 0 to 511, each once
Outputs:
- guided: float32 [512, 65536], P('pair', ('tensor', 'vocab'))
The draws below stay inside these ranges and needn't reach their ends.
Inputs may be any that keep to these rules, and one draw needn't show every extreme that they name: Every unconditional row is the partner of exactly one conditional row.
All inputs are finite; a program needn't handle non-finite values.
Results may differ from the reference program's by a relative error of at most 0.0019.
Values may be sent and summed in bfloat16 or wider, within the bound.
A program may use at most 64 MiB of HBM per device.

```python
import jax
import jax.numpy as jnp
from jax import lax

D = 8192
V = 65536
ROWS = 512


def draw_residual(key, part):
    key = jax.random.fold_in(key, 11)
    first, second = jax.random.split(key, 2)
    column = 1.0 + 2.0 * jnp.arange(D, dtype=jnp.float32) / D
    row_scale = jnp.exp(jax.random.uniform(second, (2, ROWS, 1), jnp.float32, 0.0, 2.5))
    base = jax.random.normal(first, (2, ROWS, D), jnp.float32)
    return (base * row_scale * column).astype(jnp.bfloat16)


def draw_head_weight(key, part):
    key = jax.random.fold_in(key, 23)
    first = jax.random.fold_in(key, 0)
    base = jax.random.normal(first, (D, V), jnp.float32) * (1.5 / jnp.sqrt(jnp.float32(D)))
    return base.astype(jnp.bfloat16)


def block_scale(key, extent, pieces, least, top_value):
    factor_of = 1.0
    for axis_at, shards_of in pieces:
        heights = jax.random.uniform(jax.random.fold_in(jax.random.fold_in(key, 6), axis_at), (shards_of,), jnp.float32, least / len(pieces), top_value / len(pieces))
        factor_of = factor_of * jnp.repeat(jnp.exp(heights), extent[axis_at] // shards_of).reshape((-1,) + (1,) * (len(extent) - 1 - axis_at))
    return factor_of


def noise(rng, extent, width, reach, shards=(), kind=jnp.bfloat16):
    values = jax.random.normal(rng, extent, jnp.float32) * width
    if len(shards) > 0:
        values = block_scale(rng, extent, shards, -0.22, 0.18) * values
    return jnp.clip(values, min=-reach, max=reach).astype(kind)


def setup_inputs(seed: int = 0) -> dict:
    keys = jax.random.split(jax.random.key(seed), 7)
    return {
        "context": noise(keys[0], (2, ROWS, D), 1.0, 6.0, ((0, 2), (1, 16), (2, 16))),
        "residual": draw_residual(jax.random.fold_in(keys[6], 71), 0),
        "out_weight": noise(keys[2], (D, D), D ** -0.5, 0.0625, ((0, 16), (1, 16))),
        "norm_gain": jnp.clip(1.0 + 0.18 * jax.random.normal(keys[3], (D,), jnp.float32), 0.1, 1.9),
        "head_weight": draw_head_weight(jax.random.fold_in(keys[6], 71), 0),
        "partner": jax.random.permutation(keys[5], ROWS).astype(jnp.int32),
    }


def reference(context, residual, out_weight, norm_gain, head_weight, partner):
    attn = jnp.einsum('grd,de->gre', context.astype(jnp.float32), out_weight.astype(jnp.float32))
    hidden = residual.astype(jnp.float32) + attn
    scale = lax.rsqrt(lax.optimization_barrier(jnp.mean(hidden * hidden, axis=-1, keepdims=True)) + 1e-05)
    normed = (hidden * scale * norm_gain).astype(jnp.bfloat16)
    cond_logits = jnp.dot(normed[0], head_weight, preferred_element_type=jnp.float32)
    uncond_logits = jnp.dot(normed[1], head_weight, preferred_element_type=jnp.float32)
    matched = jnp.take(uncond_logits, partner.astype(jnp.int32), axis=0)
    mixed = matched + 3.0 * (cond_logits - matched)
    top = lax.optimization_barrier(jnp.max(mixed, axis=-1, keepdims=True))
    total = lax.optimization_barrier(jnp.sum(jnp.exp(mixed - top), axis=-1, keepdims=True))
    return mixed - top - jnp.log(total)
```

```python
import jax
import jax.numpy as jnp
from jax import lax
from jax.sharding import PartitionSpec as P

D = 8192


def log_sum_exp(values, axis):
    top = jnp.max(values, axis=axis)
    return top + jnp.log(jnp.sum(jnp.exp(values - jnp.expand_dims(top, axis)), axis=axis))


def shards(context, residual, out_weight, norm_gain, head_weight, partner):
    pair = lax.axis_index("pair")
    tensor = lax.axis_index("tensor")
    context_all = lax.all_gather(context[0], "vocab", axis=0, tiled=True)
    rows = context_all.shape[0]
    mine = residual.shape[1]
    order = jnp.where(pair == 1, partner, jnp.arange(rows, dtype=partner.dtype))
    select = (order[:, None] == jnp.arange(rows, dtype=order.dtype)[None, :]).astype(jnp.bfloat16)
    arranged = jnp.dot(select, context_all, preferred_element_type=jnp.float32).astype(jnp.bfloat16)
    own = tensor * mine + jnp.arange(mine, dtype=order.dtype)
    place = (order[:, None] == own[None, :]).astype(jnp.bfloat16)
    partial = jnp.dot(arranged, out_weight, preferred_element_type=jnp.float32)
    partial = partial + jnp.dot(place, residual[0], preferred_element_type=jnp.float32)
    width = partial.shape[1]
    shares = rows // mine
    partial = partial.reshape(2, shares, mine // 2, width).transpose(1, 0, 2, 3).reshape(rows, width)
    hidden = lax.psum_scatter(partial, "tensor", scatter_dimension=0, tiled=True)
    squares = lax.psum(jnp.sum(hidden * hidden, axis=1), "vocab")
    normed = hidden * lax.rsqrt(squares / D + 1e-05)[:, None] * norm_gain
    both = lax.all_to_all(normed.reshape(2, mine // 2, width), "pair", split_axis=0, concat_axis=0, tiled=True)
    mixed_rows = (both[1] + 3.0 * (both[0] - both[1])).astype(jnp.bfloat16)
    gathered = lax.all_gather(mixed_rows, "tensor", axis=0, tiled=True)
    gathered = lax.all_gather(gathered, "vocab", axis=1, tiled=True)
    mixed = jnp.dot(gathered, head_weight, preferred_element_type=jnp.float32)
    level = log_sum_exp(mixed, 1)
    level = log_sum_exp(lax.all_gather(level, "vocab"), 0)
    level = log_sum_exp(lax.all_gather(level, "tensor"), 0)
    return mixed - level[:, None]


def solution(mesh):
    return jax.shard_map(
        shards,
        mesh=mesh,
        in_specs=(
            P("pair", "vocab", "tensor"),
            P("pair", "tensor", "vocab"),
            P("tensor", "vocab"),
            P("vocab"),
            P(None, ("tensor", "vocab")),
            P(),
        ),
        out_specs=P("pair", ("tensor", "vocab")),
        check_vma=False,
    )
```
